32 devices in a mesh: branch: 2 (over core), row: 2 (over x), col: 8 (over z, y).
Axes of the slice: x: 2, y: 2, z: 4, core: 2. Of those that a mesh axis runs over, the one named last changes fastest.
Arguments:
- tokens: bfloat16 [2, 32, 256, 1152], P('branch', 'row', 'col'), may hold values from -26 to 26
- modulation: float32 [3, 1152], replicated, may hold values from -4 to 4
- wqkv: bfloat16 [1152, 3456], replicated, may hold values from -1 to 1
- w_out: bfloat16 [1152, 1152], replicated, may hold values from -0.1875 to 0.1875
- blend: float32 [32, 256], P('row', 'col'), may hold values from 0.1 to 0.6
- reach: int32 [4, 2, 8], P(None, 'row', 'col'), may hold values from 1 to 4, as said below
Outputs:
- guided: bfloat16 [32, 256, 1152], P(('row', 'branch'), 'col')
The draws below stay inside these ranges and needn't reach their ends.
Inputs may be any that keep to these rules, and one draw needn't show every extreme that they name: Each reach is at most 4, and some tile's reach on some side is exactly 4.
All inputs are finite; a program needn't handle non-finite values.
Results may differ from the reference program's by a relative error of at most 0.0067.
Values may be sent and summed in bfloat16 or wider, within the bound.
A program may use at most 192 MiB of HBM per device.

```python
import math
import jax
import jax.numpy as jnp
from jax import lax

D = 1152
HEADS = 16
HD = 72
TR = 16
TC = 32
HALO = 4
NH = 32
NW = 256
N_ROW = 2
N_COL = 8


def draw_tokens(key, part):
    key = jax.random.fold_in(key, 11)
    shape = (2, NH, NW, D)
    return jnp.clip(jax.random.normal(key, shape, jnp.float32), -6.0, 6.0).astype(jnp.bfloat16)


def draw_wqkv(key, part):
    key = jax.random.fold_in(key, 12)
    return (jnp.clip(jax.random.normal(key, (D, 3 * D), jnp.float32), -6.0, 6.0) / math.sqrt(D)).astype(jnp.bfloat16)


def draw_reach(key, part):
    key = jax.random.fold_in(key, 13)
    row_tiles = NH // TR
    col_tiles = NW // TC
    entries = jax.random.randint(key, (4 * row_tiles * col_tiles,), 1, HALO + 1, jnp.int32)
    chosen_slot = jax.random.randint(jax.random.fold_in(key, 1), (), 0, 4 * row_tiles * col_tiles, jnp.int32)
    entries = entries.at[chosen_slot].set(HALO)
    return entries.reshape(4, row_tiles, col_tiles)


def levels(rng, dims, cuts, low, high):
    gain = 1.0
    for axis_at, shards_of in cuts:
        steps = jax.random.uniform(jax.random.fold_in(jax.random.fold_in(rng, 6), axis_at), (shards_of,), jnp.float32, low / len(cuts), high / len(cuts))
        gain = gain * jnp.repeat(jnp.exp(steps), dims[axis_at] // shards_of).reshape((-1,) + (1,) * (len(dims) - 1 - axis_at))
    return gain


def gaussian(stream_key, dims, deviation, limit, kind=jnp.bfloat16):
    array = jax.random.normal(stream_key, dims, jnp.float32) * deviation
    return jnp.minimum(jnp.maximum(array, -limit), limit).astype(kind)


def setup_inputs(seed: int = 0) -> dict:
    streams_of = jax.random.split(jax.random.key(seed), 7)
    tokens = draw_tokens(jax.random.fold_in(streams_of[6], 71), 0)
    modulation = gaussian(streams_of[1], (3, D), 1.0, 4.0, jnp.float32)
    wqkv = draw_wqkv(jax.random.fold_in(streams_of[6], 71), 0)
    w_out = gaussian(streams_of[3], (D, D), D ** -0.5, 0.1875)
    blend = jnp.clip(0.1 + 0.5 * jax.random.uniform(streams_of[4], (NH, NW), jnp.float32) ** levels(streams_of[4], (NH, NW), ((0, 2), (1, 8)), -0.2, 0.2), 0.1, 0.6)
    reach = draw_reach(jax.random.fold_in(streams_of[6], 71), 0)
    return {"tokens": tokens, "modulation": modulation, "wqkv": wqkv, "w_out": w_out, "blend": blend, "reach": reach}


GUIDANCE = 4.5

def layer_norm(values, modulation):
    widened = values.astype(jnp.float32)
    centered = widened - lax.optimization_barrier(jnp.mean(widened, axis=-1, keepdims=True))
    variance = lax.optimization_barrier(jnp.mean(centered * centered, axis=-1, keepdims=True))
    scaled = centered * lax.rsqrt(variance + 1e-06)
    return (scaled * (1.0 + modulation[1]) + modulation[0]).astype(jnp.bfloat16)

def attend(queries, keys, values, allowed):
    query_count = queries.shape[0]
    key_count = keys.shape[0]
    query_heads = queries.astype(jnp.float32).reshape(query_count, HEADS, HD)
    key_heads = keys.astype(jnp.float32).reshape(key_count, HEADS, HD)
    value_heads = values.astype(jnp.float32).reshape(key_count, HEADS, HD)
    scores = jnp.einsum('qhd,khd->hqk', query_heads, key_heads) * (1.0 / math.sqrt(HD))
    if allowed is not None:
        scores = jnp.where(allowed[None, None, :], scores, -1e+30)
    row_max = lax.optimization_barrier(jnp.max(scores, axis=-1, keepdims=True))
    powers = jnp.exp(scores - row_max)
    weights = (powers / lax.optimization_barrier(jnp.sum(powers, axis=-1, keepdims=True))).astype(jnp.bfloat16)
    attended = jnp.einsum('hqk,khd->qhd', weights.astype(jnp.float32), value_heads)
    return attended.reshape(query_count, D)

def branch_output(branch_tokens, modulation, wqkv, w_out, blend, reach):
    height = TR * N_ROW
    breadth = TC * N_COL
    normed = layer_norm(branch_tokens, modulation).reshape(height * breadth, D)
    joined = jnp.dot(normed, wqkv, preferred_element_type=jnp.float32).astype(jnp.bfloat16)
    query_image = joined[:, :D].reshape(height, breadth, D)
    key_image = joined[:, D:2 * D].reshape(height, breadth, D)
    value_image = joined[:, 2 * D:].reshape(height, breadth, D)
    padding = ((HALO, HALO), (HALO, HALO), (0, 0))
    padded_keys = jnp.pad(key_image, padding)
    padded_values = jnp.pad(value_image, padding)
    zero_index = jnp.zeros((), jnp.int32)

    def one_tile(tile_index):
        row_index = (tile_index // N_COL).astype(jnp.int32)
        col_index = (tile_index % N_COL).astype(jnp.int32)
        row_start = (row_index * TR).astype(jnp.int32)
        col_start = (col_index * TC).astype(jnp.int32)
        query_tile = lax.dynamic_slice(query_image, (row_start, col_start, zero_index), (TR, TC, D))
        window_keys = lax.dynamic_slice(padded_keys, (row_start, col_start, zero_index), (TR + 2 * HALO, TC + 2 * HALO, D))
        window_values = lax.dynamic_slice(padded_values, (row_start, col_start, zero_index), (TR + 2 * HALO, TC + 2 * HALO, D))
        row_offsets = jnp.arange(TR + 2 * HALO, dtype=jnp.int32)
        col_offsets = jnp.arange(TC + 2 * HALO, dtype=jnp.int32)
        global_rows = row_start - HALO + row_offsets
        global_cols = col_start - HALO + col_offsets
        row_fine = (global_rows >= 0) & (global_rows < height)
        row_fine = row_fine & (row_offsets >= HALO - reach[0, row_index, col_index])
        row_fine = row_fine & (row_offsets < HALO + TR + reach[1, row_index, col_index])
        col_fine = (global_cols >= 0) & (global_cols < breadth)
        col_fine = col_fine & (col_offsets >= HALO - reach[2, row_index, col_index])
        col_fine = col_fine & (col_offsets < HALO + TC + reach[3, row_index, col_index])
        allowed = (row_fine[:, None] & col_fine[None, :]).reshape(-1)
        return attend(query_tile.reshape(TR * TC, D), window_keys.reshape(-1, D), window_values.reshape(-1, D), allowed)
    tiles = lax.map(one_tile, jnp.arange(N_ROW * N_COL, dtype=jnp.int32))
    window_out = tiles.reshape(N_ROW, N_COL, TR, TC, D).transpose(0, 2, 1, 3, 4).reshape(height, breadth, D)

    def phases(image):
        return image.reshape(TR, N_ROW, TC, N_COL, D).transpose(1, 3, 0, 2, 4).reshape(N_ROW * N_COL, TR * TC, D)

    def one_phase(triple):
        return attend(triple[0], triple[1], triple[2], None).astype(jnp.bfloat16)
    lattice_out = lax.map(one_phase, (phases(query_image), phases(key_image), phases(value_image)))
    dilated_out = lattice_out.reshape(N_ROW, N_COL, TR, TC, D).transpose(2, 0, 3, 1, 4).reshape(height, breadth, D)
    weight = blend[:, :, None]
    mixed = (weight * window_out + (1.0 - weight) * dilated_out.astype(jnp.float32)).astype(jnp.bfloat16)
    projected = jnp.dot(mixed.reshape(height * breadth, D), w_out, preferred_element_type=jnp.float32)
    result = branch_tokens.astype(jnp.float32).reshape(height * breadth, D) + modulation[2] * projected
    return result.reshape(height, breadth, D)

def reference(tokens, modulation, wqkv, w_out, blend, reach):
    uncond = branch_output(tokens[0], modulation, wqkv, w_out, blend, reach)
    cond = branch_output(tokens[1], modulation, wqkv, w_out, blend, reach)
    return ((1.0 - GUIDANCE) * uncond + GUIDANCE * cond).astype(jnp.bfloat16)
```

```python
import functools
import math

import jax
import jax.numpy as jnp
import numpy as np
from jax import lax
from jax.experimental import pallas as pl
from jax.experimental.pallas import tpu as pltpu
from jax.sharding import PartitionSpec as P

HEADS = 16
HALO = 4


GUIDANCE = 4.5


def with_halo(cells, sides, width):
    for axis, dim in sides:
        count = lax.axis_size(axis)
        ends = count - 1
        head = lax.slice_in_dim(cells, 0, width, axis=dim)
        tail = lax.slice_in_dim(cells, cells.shape[dim] - width, cells.shape[dim], axis=dim)
        cells = jnp.concatenate(
            [
                lax.ppermute(tail, axis, [(i, (i + 1) % count) for i in range(ends)]),
                cells,
                lax.ppermute(head, axis, [((i + 1) % count, i) for i in range(ends)]),
            ],
            axis=dim,
        )
    return cells


def layer_norm(values, modulation):
    widened = values.astype(jnp.float32)
    centered = widened - jnp.mean(widened, axis=-1, keepdims=True)
    variance = jnp.mean(centered * centered, axis=-1, keepdims=True)
    scaled = centered * lax.rsqrt(variance + 1e-06)
    return (scaled * (1.0 + modulation[1]) + modulation[0]).astype(jnp.bfloat16)


def project(normed, wqkv):
    feature_width = normed.shape[-1]
    joined = jnp.dot(normed, wqkv, preferred_element_type=jnp.float32).astype(jnp.bfloat16)
    return (
        joined[:, :feature_width],
        joined[:, feature_width : 2 * feature_width],
        joined[:, 2 * feature_width :],
    )


def attend(queries, keys, values, allowed):
    query_count, feature_width = queries.shape
    key_count = keys.shape[0]
    head_size = feature_width // HEADS
    query_heads = queries.reshape(query_count, HEADS, head_size)
    key_heads = keys.reshape(key_count, HEADS, head_size)
    value_heads = values.reshape(key_count, HEADS, head_size)
    scores = jnp.einsum(
        "qhd,khd->hqk", query_heads, key_heads, preferred_element_type=jnp.float32
    ) * (1.0 / math.sqrt(head_size))
    if allowed is not None:
        scores = jnp.where(allowed[None, None, :], scores, -1e30)
    row_max = jnp.max(scores, axis=-1, keepdims=True)
    powers = jnp.exp(scores - row_max)
    weights = (powers / jnp.sum(powers, axis=-1, keepdims=True)).astype(jnp.bfloat16)
    attended = jnp.einsum("hqk,khd->qhd", weights, value_heads, preferred_element_type=jnp.float32)
    return attended.reshape(query_count, feature_width)


def window_mask(reach, rows, cols):
    row_start = lax.axis_index("row") * rows
    col_start = lax.axis_index("col") * cols
    height = rows * lax.axis_size("row")
    breadth = cols * lax.axis_size("col")
    row_offsets = jnp.arange(rows + 2 * HALO, dtype=jnp.int32)
    col_offsets = jnp.arange(cols + 2 * HALO, dtype=jnp.int32)
    global_rows = row_start - HALO + row_offsets
    global_cols = col_start - HALO + col_offsets
    row_fine = (global_rows >= 0) & (global_rows < height)
    row_fine = (
        row_fine
        & (row_offsets >= HALO - reach[0, 0, 0])
        & (row_offsets < HALO + rows + reach[1, 0, 0])
    )
    col_fine = (global_cols >= 0) & (global_cols < breadth)
    col_fine = (
        col_fine
        & (col_offsets >= HALO - reach[2, 0, 0])
        & (col_offsets < HALO + cols + reach[3, 0, 0])
    )
    return (row_fine[:, None] & col_fine[None, :]).reshape(-1)


def on_device(tokens, modulation, wqkv, w_out, blend, reach):
    rows, cols, feature_width = (tokens.shape[1], tokens.shape[2], tokens.shape[3])
    row_groups = lax.axis_size("row")
    col_groups = lax.axis_size("col")
    sub_rows = rows // row_groups
    sub_cols = cols // col_groups
    normed = layer_norm(tokens[0], modulation).reshape(rows * cols, feature_width)
    queries, keys, values = project(normed, wqkv)
    stacked = jnp.stack(
        (keys.reshape(rows, cols, feature_width), values.reshape(rows, cols, feature_width)), axis=0
    )
    window = with_halo(stacked, (("row", 1), ("col", 2)), HALO)
    allowed = window_mask(reach, rows, cols)
    window_out = attend(
        queries, window[0].reshape(-1, feature_width), window[1].reshape(-1, feature_width), allowed
    )
    split = jnp.stack((queries, keys, values), axis=0).reshape(
        -1, sub_rows, row_groups, sub_cols, col_groups, feature_width
    )
    outgoing = split.transpose(0, 2, 4, 1, 3, 5).reshape(
        -1, row_groups, col_groups, sub_rows * sub_cols, feature_width
    )
    carried = outgoing.shape[0]
    flat_out = outgoing.reshape(
        carried, row_groups * col_groups, sub_rows * sub_cols, feature_width
    )
    arrived = lax.all_to_all(flat_out, ("row", "col"), split_axis=1, concat_axis=1, tiled=True)
    arrived = arrived.reshape(carried, rows * cols, feature_width)
    lattice_queries, lattice_keys, lattice_values = (arrived[0], arrived[1], arrived[2])
    lattice_out = attend(lattice_queries, lattice_keys, lattice_values, None).astype(jnp.bfloat16)
    joint_in = lattice_out.reshape(row_groups * col_groups, sub_rows * sub_cols, feature_width)
    returned = lax.all_to_all(joint_in, ("row", "col"), split_axis=0, concat_axis=0, tiled=True)
    returned = returned.reshape(row_groups, col_groups, sub_rows, sub_cols, feature_width)
    dilated_out = returned.transpose(2, 0, 3, 1, 4).reshape(rows * cols, feature_width)
    weight = blend.reshape(rows * cols, 1)
    mixed = (weight * window_out + (1.0 - weight) * dilated_out.astype(jnp.float32)).astype(
        jnp.bfloat16
    )
    projected = jnp.dot(mixed, w_out, preferred_element_type=jnp.float32)
    branch_out = (
        tokens[0].reshape(rows * cols, feature_width).astype(jnp.float32)
        + modulation[2] * projected
    )
    coefficient = jnp.where(lax.axis_index("branch") == 1, GUIDANCE, 1.0 - GUIDANCE)
    branch_term = (coefficient * branch_out).reshape(rows, cols, feature_width)
    guided = lax.psum_scatter(branch_term, "branch", scatter_dimension=0, tiled=True)
    return guided.astype(jnp.bfloat16)


MESH = pl.DeviceIdType.MESH
LANES = 128
CHUNK = 128


def halo_slots(rows, cols):
    side, edge, corner = HALO * cols, rows * HALO, HALO * HALO
    sizes = [(side, 1, 0), (edge, 0, -1), (edge, 0, 1), (corner, 1, -1), (corner, 1, 1)]
    slots, start = [], 0
    for count, flip, step in sizes:
        slots.append((start, count, flip, step))
        start += count
    return slots, start


def selections(rows, cols, row_groups, col_groups, padded):
    tile = rows * cols
    sub_rows, sub_cols = rows // row_groups, cols // col_groups
    natural = np.arange(tile).reshape(sub_rows, row_groups, sub_cols, col_groups)
    phased = natural.transpose(1, 3, 0, 2).reshape(-1)
    grid = np.arange(tile).reshape(rows, cols)
    slots, total = halo_slots(rows, cols)
    chosen = [phased]
    offsets = []
    for row in range(2):
        sent, where = [], []
        for _, count, flip, step in slots:
            picked = grid
            if flip:
                picked = picked[rows - HALO :] if row == 0 else picked[:HALO]
            if step:
                picked = picked[:, :HALO] if step < 0 else picked[:, cols - HALO :]
            sent.append(picked.reshape(-1))
            r = np.arange(rows)
            if flip:
                r = np.arange(rows, rows + HALO) if row == 0 else np.arange(-HALO, 0)
            c = np.arange(cols)
            if step:
                c = np.arange(cols, cols + HALO) if step < 0 else np.arange(-HALO, 0)
            rr, cc = np.meshgrid(r, c, indexing="ij")
            where.append(np.stack([rr.reshape(-1), cc.reshape(-1)], axis=1))
        chosen.append(np.concatenate(sent))
        spread = np.full((padded, 2), -1000, np.int32)
        spread[:total] = np.concatenate(where)
        offsets.append(spread)
    chosen = np.concatenate(chosen)
    select = (chosen[:, None] == np.arange(tile)[None, :]).astype(np.float32)
    half = tile // 2
    per = tile // (row_groups * col_groups)
    front = phased.reshape(row_groups * col_groups, per)[:, : per // 2].reshape(-1)
    restore = (front[None, :] == np.arange(half)[:, None]).astype(np.float32)
    return select, restore, np.concatenate(offsets)


def fused(
    dims,
    x_ref, mod_ref, w_ref, wout_ref, blend_ref, reach_ref, select_ref, restore_ref, offs_ref,
    out_ref,
    normed, phased, halo_out, halo_in, lattice, near, far,
    dil, dil_other, combined, returned, win, win_other, rest,
    a2a_send, a2a_recv, halo_send, halo_recv, ret_send, ret_recv, pair_send, pair_recv,
):
    rows, cols, row_groups, col_groups = dims
    tile = rows * cols
    half = tile // 2
    groups = row_groups * col_groups
    width = x_ref.shape[-1]
    size = width // HEADS
    slots, sent = halo_slots(rows, cols)
    padded = halo_in.shape[0]
    branch = lax.axis_index("branch")
    row = lax.axis_index("row")
    col = lax.axis_index("col")
    me = row * col_groups + col
    other = 1 - branch

    def place(p):
        return (branch, p // col_groups, p % col_groups)

    barrier = pltpu.get_barrier_semaphore()

    def greet(k, carry):
        pl.semaphore_signal(
            barrier, inc=1, device_id=place((me + k) % groups), device_id_type=MESH
        )
        return carry

    lax.fori_loop(1, groups, greet, 0)
    pl.semaphore_signal(barrier, inc=1, device_id=(other, row, col), device_id_type=MESH)

    gain = 1.0 + mod_ref[1:2, :]
    shift = mod_ref[0:1, :]

    def norm(i, carry):
        at = pl.ds(pl.multiple_of(i * CHUNK, CHUNK), CHUNK)
        widened = x_ref[at, :].astype(jnp.float32)
        centered = widened - jnp.mean(widened, axis=-1, keepdims=True)
        variance = jnp.mean(centered * centered, axis=-1, keepdims=True)
        scaled = centered * lax.rsqrt(variance + 1e-06)
        normed[at, :] = (scaled * gain + shift).astype(jnp.bfloat16)
        return carry

    lax.fori_loop(0, tile // CHUNK, norm, 0)

    start = pl.multiple_of(tile + row * sent, 16)
    halo_out[...] = jnp.dot(
        select_ref[pl.ds(start, sent), :], normed[...], preferred_element_type=jnp.float32
    ).astype(jnp.bfloat16)

    pl.semaphore_wait(barrier, groups)

    def pair_copy(k, source, target):
        return pltpu.make_async_remote_copy(
            src_ref=source, dst_ref=target, send_sem=pair_send.at[k], recv_sem=pair_recv.at[k],
            device_id=(other, row, col), device_id_type=MESH,
        )

    halo_copies = []
    for k, (begin, count, flip, step) in enumerate(slots):
        to = (
            branch,
            (row + flip) % row_groups,
            (col + step + col_groups) % col_groups,
        )
        copy = pltpu.make_async_remote_copy(
            src_ref=halo_out.at[pl.ds(begin, count)], dst_ref=halo_in.at[pl.ds(begin, count)],
            send_sem=halo_send.at[k], recv_sem=halo_recv.at[k],
            device_id=to, device_id_type=MESH,
        )
        copy.start()
        halo_copies.append(copy)

    per = tile // groups
    blocks = CHUNK // per

    def arrange(i, carry):
        at = pl.ds(pl.multiple_of(i * CHUNK, CHUNK), CHUNK)
        picked = jnp.dot(select_ref[at, :], normed[...], preferred_element_type=jnp.float32)
        phased[pl.ds(i * blocks, blocks)] = picked.astype(jnp.bfloat16).reshape(blocks, per, width)
        return carry

    lax.fori_loop(0, tile // CHUNK, arrange, 0)

    def outward(k):
        to = (me + k) % groups
        return pltpu.make_async_remote_copy(
            src_ref=phased.at[to], dst_ref=lattice.at[me],
            send_sem=a2a_send.at[k], recv_sem=a2a_recv.at[k],
            device_id=place(to), device_id_type=MESH,
        )

    def inward(k):
        return pltpu.make_async_remote_copy(
            src_ref=phased.at[me], dst_ref=lattice.at[(me + groups - k) % groups],
            send_sem=a2a_send.at[k], recv_sem=a2a_recv.at[k],
            device_id=place((me + k) % groups), device_id_type=MESH,
        )

    def send_out(k, carry):
        outward(k).start()
        return carry

    lax.fori_loop(1, groups, send_out, 0)
    tokens_copy = pair_copy(0, x_ref.at[pl.ds(pl.multiple_of(other * half, half), half)], rest)
    tokens_copy.start()
    lattice[me] = phased[me]

    log_scale = math.log2(math.e) / math.sqrt(size)
    lane = lax.broadcasted_iota(jnp.int32, (1, LANES), 1)

    def clear(ref, begin, count, weight):
        mark = jnp.where(lane == size, weight, 0.0).astype(jnp.bfloat16)
        mark = jnp.broadcast_to(mark, (count, LANES))
        blank = jnp.zeros((count, LANES), jnp.bfloat16)

        def body(h, carry):
            at = pl.ds(begin, count)
            if begin == 0:
                ref[h, at, :] = blank
            ref[HEADS + h, at, :] = blank
            ref[2 * HEADS + h, at, :] = mark
            return carry

        lax.fori_loop(0, HEADS, body, 0)

    def spread(ref, part, at, value):
        value = value.astype(jnp.bfloat16)
        for h in range(HEADS):
            ref[part * HEADS + h, at, 0:size] = value[:, h * size : (h + 1) * size]

    def weights_of(part):
        return w_ref[:, pl.ds(pl.multiple_of(part * width, LANES), width)]

    piece = 2 * CHUNK

    def project_all(ref, load):
        clear(ref, 0, tile, jnp.ones((1, 1), jnp.float32))

        def body(step, carry):
            part = step // (tile // piece)
            i = step % (tile // piece)
            at = pl.ds(pl.multiple_of(i * piece, piece), piece)
            y = jnp.dot(load(i, at), weights_of(part), preferred_element_type=jnp.float32)
            factor = jnp.where(part == 0, log_scale, 1.0)
            spread(ref, part, at, y * factor)
            return carry

        lax.fori_loop(0, 3 * (tile // piece), body, 0)

    wide = piece // per
    project_all(near, lambda i, at: phased[pl.ds(i * wide, wide)].reshape(piece, width))

    offset_at = pl.ds(pl.multiple_of(row * padded, padded), padded)
    r_off = offs_ref[offset_at, 0:1]
    c_off = offs_ref[offset_at, 1:2]
    left = jnp.where(col == 0, 0, reach_ref[2])
    right = jnp.where(col == col_groups - 1, 0, reach_ref[3])
    allowed = (
        (r_off >= -reach_ref[0])
        & (r_off < rows + reach_ref[1])
        & (c_off >= -left)
        & (c_off < cols + right)
    )
    allow = jnp.where(allowed, 1.0, 0.0)
    halo_in[sent:padded, :] = jnp.zeros((padded - sent, width), jnp.bfloat16)
    clear(near, tile, padded, allow)
    for copy in halo_copies:
        copy.wait_recv()
    halo_at = pl.ds(tile, padded)

    def project_halo(part, carry):
        weight = weights_of(part)
        y = jnp.dot(halo_in[...], weight, preferred_element_type=jnp.float32)
        spare = jnp.dot(normed[0:16, :], weight, preferred_element_type=jnp.float32)[0:1, :]
        spare = spare * jnp.where(part == 1, 1.0, 0.0)
        spread(near, part, halo_at, jnp.where(allow > 0.5, y, spare))
        return carry

    lax.fori_loop(1, 3, project_halo, 0)

    def attend_heads(ref, first, last):
        def body(h, carry):
            keys = ref[HEADS + h]
            values = ref[2 * HEADS + h]
            for r in range(tile // CHUNK):
                at = pl.ds(r * CHUNK, CHUNK)
                scores = lax.dot_general(
                    ref[h, at, :], keys, (((1,), (1,)), ((), ())),
                    preferred_element_type=jnp.float32,
                )
                powers = jnp.exp2(scores - jnp.max(scores, axis=-1, keepdims=True))
                got = jnp.dot(
                    powers.astype(jnp.bfloat16), values, preferred_element_type=jnp.float32
                )
                ref[h, at, :] = (got * (1.0 / got[:, size : size + 1])).astype(jnp.bfloat16)
            return carry

        lax.fori_loop(first, last, body, 0)

    def gather_heads(ref, target):
        count = target.shape[0] * CHUNK // tile

        def body(i, carry):
            at = pl.ds(pl.multiple_of(i * CHUNK, CHUNK), CHUNK)
            to = pl.ds(i * count, count)
            for h in range(HEADS):
                value = ref[h, at, 0:size].reshape(count, 2, per // 2, size)
                target[to, :, :, h * size : (h + 1) * size] = value
            return carry

        lax.fori_loop(0, tile // CHUNK, body, 0)

    attend_heads(near, 0, HEADS // 2)

    def take_in(k, carry):
        inward(k).wait_recv()
        return carry

    lax.fori_loop(1, groups, take_in, 0)
    project_all(far, lambda i, at: lattice[pl.ds(i * wide, wide)].reshape(piece, width))
    attend_heads(far, 0, HEADS)
    gather_heads(far, dil)
    dil_copy = pair_copy(1, dil.at[:, other], dil_other)
    dil_copy.start()
    dil_copy.wait_recv()
    mine = jnp.where(branch == 1, GUIDANCE, 1.0 - GUIDANCE)
    theirs = 1.0 - mine

    def combine(i, carry):
        combined[i] = (
            mine * dil[i, branch].astype(jnp.float32) + theirs * dil_other[i].astype(jnp.float32)
        ).astype(jnp.bfloat16)
        return carry

    lax.fori_loop(0, groups, combine, 0)

    def back(k):
        to = (me + k) % groups
        return pltpu.make_async_remote_copy(
            src_ref=combined.at[to], dst_ref=returned.at[me],
            send_sem=ret_send.at[k], recv_sem=ret_recv.at[k],
            device_id=place(to), device_id_type=MESH,
        )

    def back_in(k):
        return pltpu.make_async_remote_copy(
            src_ref=combined.at[me], dst_ref=returned.at[(me + groups - k) % groups],
            send_sem=ret_send.at[k], recv_sem=ret_recv.at[k],
            device_id=place((me + k) % groups), device_id_type=MESH,
        )

    def send_back(k, carry):
        back(k).start()
        return carry

    lax.fori_loop(1, groups, send_back, 0)
    returned[me] = combined[me]

    attend_heads(near, HEADS // 2, HEADS)
    gather_heads(near, win)
    win_copy = pair_copy(2, win.at[:, other], win_other)
    win_copy.start()

    def take_back(k, carry):
        back_in(k).wait_recv()
        return carry

    lax.fori_loop(1, groups, take_back, 0)
    win_copy.wait_recv()
    tokens_copy.wait_recv()

    weight = blend_ref[pl.ds(pl.multiple_of(branch * half, half), half), :]
    window = mine * win[:, branch].astype(jnp.float32) + theirs * win_other[...].astype(jnp.float32)
    window = window.reshape(half, width)
    dilated = returned[...].astype(jnp.float32).reshape(half, width)
    mixed = (weight * window + (1.0 - weight) * dilated).astype(jnp.bfloat16)
    mixed = jnp.dot(restore_ref[...], mixed, preferred_element_type=jnp.float32)
    projected = jnp.dot(
        mixed.astype(jnp.bfloat16), wout_ref[...], preferred_element_type=jnp.float32
    )
    own = x_ref[pl.ds(pl.multiple_of(branch * half, half), half), :].astype(jnp.float32)
    base = mine * own + theirs * rest[...].astype(jnp.float32)
    out_ref[...] = (base + mod_ref[2:3, :] * projected).astype(jnp.bfloat16)

    for copy in halo_copies:
        copy.wait_send()
    for copy in (tokens_copy, dil_copy, win_copy):
        copy.wait_send()

    def finish(k, carry):
        outward(k).wait_send()
        back(k).wait_send()
        return carry

    lax.fori_loop(1, groups, finish, 0)


def on_device_fused(dims, tokens, modulation, wqkv, w_out, blend, reach):
    rows, cols, row_groups, col_groups = dims
    tile = rows * cols
    half = tile // 2
    groups = row_groups * col_groups
    per = tile // groups
    width = tokens.shape[-1]
    _, sent = halo_slots(rows, cols)
    padded = -(-(tile + sent) // LANES) * LANES - tile
    select, restore, offsets = selections(rows, cols, row_groups, col_groups, padded)
    order = blend.reshape(2, rows // row_groups // 2, row_groups, cols // col_groups, col_groups)
    order = order.transpose(0, 2, 4, 1, 3).reshape(tile, 1)
    bf16 = jnp.bfloat16
    vmem = pl.BlockSpec(memory_space=pltpu.VMEM)
    out = pl.pallas_call(
        functools.partial(fused, dims),
        out_shape=jax.ShapeDtypeStruct((half, width), bf16),
        in_specs=[vmem] * 5 + [pl.BlockSpec(memory_space=pltpu.SMEM)] + [vmem] * 3,
        out_specs=vmem,
        scratch_shapes=[
            pltpu.VMEM((tile, width), bf16),
            pltpu.VMEM((groups, per, width), bf16),
            pltpu.VMEM((sent, width), bf16),
            pltpu.VMEM((padded, width), bf16),
            pltpu.VMEM((groups, per, width), bf16),
            pltpu.VMEM((3 * HEADS, tile + padded, LANES), bf16),
            pltpu.VMEM((3 * HEADS, tile, LANES), bf16),
            pltpu.VMEM((groups, 2, per // 2, width), bf16),
            pltpu.VMEM((groups, per // 2, width), bf16),
            pltpu.VMEM((groups, per // 2, width), bf16),
            pltpu.VMEM((groups, per // 2, width), bf16),
            pltpu.VMEM((groups, 2, per // 2, width), bf16),
            pltpu.VMEM((groups, per // 2, width), bf16),
            pltpu.VMEM((half, width), bf16),
            pltpu.SemaphoreType.DMA((groups,)),
            pltpu.SemaphoreType.DMA((groups,)),
            pltpu.SemaphoreType.DMA((5,)),
            pltpu.SemaphoreType.DMA((5,)),
            pltpu.SemaphoreType.DMA((groups,)),
            pltpu.SemaphoreType.DMA((groups,)),
            pltpu.SemaphoreType.DMA((3,)),
            pltpu.SemaphoreType.DMA((3,)),
        ],
        compiler_params=pltpu.CompilerParams(
            collective_id=0, has_side_effects=True, vmem_limit_bytes=60 * 1024 * 1024
        ),
    )(
        tokens.reshape(tile, width), modulation, wqkv, w_out, order, reach.reshape(4),
        jnp.asarray(select, bf16), jnp.asarray(restore, bf16), jnp.asarray(offsets),
    )
    return out.reshape(rows // 2, cols, width)


def solution(mesh):
    in_specs = (
        P("branch", "row", "col", None),
        P(),
        P(),
        P(),
        P("row", "col"),
        P(None, "row", "col"),
    )
    out_specs = P(("row", "branch"), "col", None)
    row_groups, col_groups = mesh.shape["row"], mesh.shape["col"]

    def whole(tokens, *others):
        rows, cols = tokens.shape[1] // row_groups, tokens.shape[2] // col_groups
        groups = row_groups * col_groups
        fits = (
            row_groups == 2
            and col_groups > 2
            and (rows * cols) % (32 * groups) == 0
            and rows // row_groups % 2 == 0
        )
        body = on_device
        if fits:
            body = functools.partial(on_device_fused, (rows, cols, row_groups, col_groups))
        return jax.shard_map(
            body, mesh=mesh, in_specs=in_specs, out_specs=out_specs, check_vma=False
        )(tokens, *others)

    return whole
```

```python
import functools
import math

import jax
import jax.numpy as jnp
import numpy as np
from jax import lax
from jax.experimental import pallas as pl
from jax.experimental.pallas import tpu as pltpu
from jax.sharding import PartitionSpec as P

HEADS = 16
HALO = 4


GUIDANCE = 4.5


def with_halo(cells, sides, width):
    for axis, dim in sides:
        count = lax.axis_size(axis)
        ends = count - 1
        head = lax.slice_in_dim(cells, 0, width, axis=dim)
        tail = lax.slice_in_dim(cells, cells.shape[dim] - width, cells.shape[dim], axis=dim)
        cells = jnp.concatenate(
            [
                lax.ppermute(tail, axis, [(i, (i + 1) % count) for i in range(ends)]),
                cells,
                lax.ppermute(head, axis, [((i + 1) % count, i) for i in range(ends)]),
            ],
            axis=dim,
        )
    return cells


def layer_norm(values, modulation):
    widened = values.astype(jnp.float32)
    centered = widened - jnp.mean(widened, axis=-1, keepdims=True)
    variance = jnp.mean(centered * centered, axis=-1, keepdims=True)
    scaled = centered * lax.rsqrt(variance + 1e-06)
    return (scaled * (1.0 + modulation[1]) + modulation[0]).astype(jnp.bfloat16)


def project(normed, wqkv):
    feature_width = normed.shape[-1]
    joined = jnp.dot(normed, wqkv, preferred_element_type=jnp.float32).astype(jnp.bfloat16)
    return (
        joined[:, :feature_width],
        joined[:, feature_width : 2 * feature_width],
        joined[:, 2 * feature_width :],
    )


def attend(queries, keys, values, allowed):
    query_count, feature_width = queries.shape
    key_count = keys.shape[0]
    head_size = feature_width // HEADS
    query_heads = queries.reshape(query_count, HEADS, head_size)
    key_heads = keys.reshape(key_count, HEADS, head_size)
    value_heads = values.reshape(key_count, HEADS, head_size)
    scores = jnp.einsum(
        "qhd,khd->hqk", query_heads, key_heads, preferred_element_type=jnp.float32
    ) * (1.0 / math.sqrt(head_size))
    if allowed is not None:
        scores = jnp.where(allowed[None, None, :], scores, -1e30)
    row_max = jnp.max(scores, axis=-1, keepdims=True)
    powers = jnp.exp(scores - row_max)
    weights = (powers / jnp.sum(powers, axis=-1, keepdims=True)).astype(jnp.bfloat16)
    attended = jnp.einsum("hqk,khd->qhd", weights, value_heads, preferred_element_type=jnp.float32)
    return attended.reshape(query_count, feature_width)


def window_mask(reach, rows, cols):
    row_start = lax.axis_index("row") * rows
    col_start = lax.axis_index("col") * cols
    height = rows * lax.axis_size("row")
    breadth = cols * lax.axis_size("col")
    row_offsets = jnp.arange(rows + 2 * HALO, dtype=jnp.int32)
    col_offsets = jnp.arange(cols + 2 * HALO, dtype=jnp.int32)
    global_rows = row_start - HALO + row_offsets
    global_cols = col_start - HALO + col_offsets
    row_fine = (global_rows >= 0) & (global_rows < height)
    row_fine = (
        row_fine
        & (row_offsets >= HALO - reach[0, 0, 0])
        & (row_offsets < HALO + rows + reach[1, 0, 0])
    )
    col_fine = (global_cols >= 0) & (global_cols < breadth)
    col_fine = (
        col_fine
        & (col_offsets >= HALO - reach[2, 0, 0])
        & (col_offsets < HALO + cols + reach[3, 0, 0])
    )
    return (row_fine[:, None] & col_fine[None, :]).reshape(-1)


def on_device(tokens, modulation, wqkv, w_out, blend, reach):
    rows, cols, feature_width = (tokens.shape[1], tokens.shape[2], tokens.shape[3])
    row_groups = lax.axis_size("row")
    col_groups = lax.axis_size("col")
    sub_rows = rows // row_groups
    sub_cols = cols // col_groups
    normed = layer_norm(tokens[0], modulation).reshape(rows * cols, feature_width)
    queries, keys, values = project(normed, wqkv)
    stacked = jnp.stack(
        (keys.reshape(rows, cols, feature_width), values.reshape(rows, cols, feature_width)), axis=0
    )
    window = with_halo(stacked, (("row", 1), ("col", 2)), HALO)
    allowed = window_mask(reach, rows, cols)
    window_out = attend(
        queries, window[0].reshape(-1, feature_width), window[1].reshape(-1, feature_width), allowed
    )
    split = jnp.stack((queries, keys, values), axis=0).reshape(
        -1, sub_rows, row_groups, sub_cols, col_groups, feature_width
    )
    outgoing = split.transpose(0, 2, 4, 1, 3, 5).reshape(
        -1, row_groups, col_groups, sub_rows * sub_cols, feature_width
    )
    carried = outgoing.shape[0]
    flat_out = outgoing.reshape(
        carried, row_groups * col_groups, sub_rows * sub_cols, feature_width
    )
    arrived = lax.all_to_all(flat_out, ("row", "col"), split_axis=1, concat_axis=1, tiled=True)
    arrived = arrived.reshape(carried, rows * cols, feature_width)
    lattice_queries, lattice_keys, lattice_values = (arrived[0], arrived[1], arrived[2])
    lattice_out = attend(lattice_queries, lattice_keys, lattice_values, None).astype(jnp.bfloat16)
    joint_in = lattice_out.reshape(row_groups * col_groups, sub_rows * sub_cols, feature_width)
    returned = lax.all_to_all(joint_in, ("row", "col"), split_axis=0, concat_axis=0, tiled=True)
    returned = returned.reshape(row_groups, col_groups, sub_rows, sub_cols, feature_width)
    dilated_out = returned.transpose(2, 0, 3, 1, 4).reshape(rows * cols, feature_width)
    weight = blend.reshape(rows * cols, 1)
    mixed = (weight * window_out + (1.0 - weight) * dilated_out.astype(jnp.float32)).astype(
        jnp.bfloat16
    )
    projected = jnp.dot(mixed, w_out, preferred_element_type=jnp.float32)
    branch_out = (
        tokens[0].reshape(rows * cols, feature_width).astype(jnp.float32)
        + modulation[2] * projected
    )
    coefficient = jnp.where(lax.axis_index("branch") == 1, GUIDANCE, 1.0 - GUIDANCE)
    branch_term = (coefficient * branch_out).reshape(rows, cols, feature_width)
    guided = lax.psum_scatter(branch_term, "branch", scatter_dimension=0, tiled=True)
    return guided.astype(jnp.bfloat16)


MESH = pl.DeviceIdType.MESH
LANES = 128
CHUNK = 128


def halo_slots(rows, cols):
    side, edge, corner = HALO * cols, rows * HALO, HALO * HALO
    sizes = [(side, 1, 0), (edge, 0, -1), (edge, 0, 1), (corner, 1, -1), (corner, 1, 1)]
    slots, start = [], 0
    for count, flip, step in sizes:
        slots.append((start, count, flip, step))
        start += count
    return slots, start


def selections(rows, cols, row_groups, col_groups, padded):
    tile = rows * cols
    sub_rows, sub_cols = rows // row_groups, cols // col_groups
    natural = np.arange(tile).reshape(sub_rows, row_groups, sub_cols, col_groups)
    phased = natural.transpose(1, 3, 0, 2).reshape(-1)
    grid = np.arange(tile).reshape(rows, cols)
    slots, total = halo_slots(rows, cols)
    chosen = [phased]
    offsets = []
    for row in range(2):
        sent, where = [], []
        for _, count, flip, step in slots:
            picked = grid
            if flip:
                picked = picked[rows - HALO :] if row == 0 else picked[:HALO]
            if step:
                picked = picked[:, :HALO] if step < 0 else picked[:, cols - HALO :]
            sent.append(picked.reshape(-1))
            r = np.arange(rows)
            if flip:
                r = np.arange(rows, rows + HALO) if row == 0 else np.arange(-HALO, 0)
            c = np.arange(cols)
            if step:
                c = np.arange(cols, cols + HALO) if step < 0 else np.arange(-HALO, 0)
            rr, cc = np.meshgrid(r, c, indexing="ij")
            where.append(np.stack([rr.reshape(-1), cc.reshape(-1)], axis=1))
        chosen.append(np.concatenate(sent))
        spread = np.full((padded, 2), -1000, np.int32)
        spread[:total] = np.concatenate(where)
        offsets.append(spread)
    chosen = np.concatenate(chosen)
    select = (chosen[:, None] == np.arange(tile)[None, :]).astype(np.float32)
    half = tile // 2
    per = tile // (row_groups * col_groups)
    front = phased.reshape(row_groups * col_groups, per)[:, : per // 2].reshape(-1)
    restore = (front[None, :] == np.arange(half)[:, None]).astype(np.float32)
    offsets.append(np.stack([front // cols, front % cols], axis=1).astype(np.int32))
    return select, restore, np.concatenate(offsets)


def fused(
    dims,
    x_ref, mod_ref, w_hbm, wout_hbm, blend_ref, reach_ref, select_ref, restore_ref, offs_ref,
    out_ref,
    normed, phased, halo_out, halo_in, lattice, near, far,
    dil, dil_other, combined, returned, win, win_other, rest,
    w_ref, wout_ref, scores_a, scores_b, heads_out, load_sem,
    a2a_send, a2a_recv, halo_send, halo_recv, ret_send, ret_recv, pair_send, pair_recv,
):
    rows, cols, row_groups, col_groups = dims
    tile = rows * cols
    half = tile // 2
    groups = row_groups * col_groups
    width = x_ref.shape[-1]
    size = width // HEADS
    slots, sent = halo_slots(rows, cols)
    padded = halo_in.shape[0]
    branch = lax.axis_index("branch")
    row = lax.axis_index("row")
    col = lax.axis_index("col")
    me = row * col_groups + col
    other = 1 - branch

    def place(p):
        return (branch, p // col_groups, p % col_groups)

    w_copy = pltpu.make_async_copy(w_hbm, w_ref, load_sem.at[0])
    w_copy.start()
    wout_copy = pltpu.make_async_copy(wout_hbm, wout_ref, load_sem.at[1])
    wout_copy.start()

    barrier = pltpu.get_barrier_semaphore()

    def greet(k, carry):
        pl.semaphore_signal(
            barrier, inc=1, device_id=place((me + k) % groups), device_id_type=MESH
        )
        return carry

    lax.fori_loop(1, groups, greet, 0)
    pl.semaphore_signal(barrier, inc=1, device_id=(other, row, col), device_id_type=MESH)

    gain = 1.0 + mod_ref[1:2, :]
    shift = mod_ref[0:1, :]

    def norm(i, carry):
        at = pl.ds(pl.multiple_of(i * CHUNK, CHUNK), CHUNK)
        widened = x_ref[at, :].astype(jnp.float32)
        centered = widened - jnp.mean(widened, axis=-1, keepdims=True)
        variance = jnp.mean(centered * centered, axis=-1, keepdims=True)
        scaled = centered * lax.rsqrt(variance + 1e-06)
        normed[at, :] = (scaled * gain + shift).astype(jnp.bfloat16)
        return carry

    lax.fori_loop(0, tile // CHUNK, norm, 0)

    start = pl.multiple_of(tile + row * sent, 16)
    halo_out[...] = jnp.dot(
        select_ref[pl.ds(start, sent), :], normed[...], preferred_element_type=jnp.float32
    ).astype(jnp.bfloat16)

    pl.semaphore_wait(barrier, groups)

    def pair_copy(k, source, target):
        return pltpu.make_async_remote_copy(
            src_ref=source, dst_ref=target, send_sem=pair_send.at[k], recv_sem=pair_recv.at[k],
            device_id=(other, row, col), device_id_type=MESH,
        )

    halo_copies = []
    for k, (begin, count, flip, step) in enumerate(slots):
        to = (
            branch,
            (row + flip) % row_groups,
            (col + step + col_groups) % col_groups,
        )
        copy = pltpu.make_async_remote_copy(
            src_ref=halo_out.at[pl.ds(begin, count)], dst_ref=halo_in.at[pl.ds(begin, count)],
            send_sem=halo_send.at[k], recv_sem=halo_recv.at[k],
            device_id=to, device_id_type=MESH,
        )
        copy.start()
        halo_copies.append(copy)

    per = tile // groups
    blocks = CHUNK // per

    def arrange(i, carry):
        at = pl.ds(pl.multiple_of(i * CHUNK, CHUNK), CHUNK)
        picked = jnp.dot(select_ref[at, :], normed[...], preferred_element_type=jnp.float32)
        phased[pl.ds(i * blocks, blocks)] = picked.astype(jnp.bfloat16).reshape(blocks, per, width)
        return carry

    lax.fori_loop(0, tile // CHUNK, arrange, 0)

    def outward(k):
        to = (me + k) % groups
        return pltpu.make_async_remote_copy(
            src_ref=phased.at[to], dst_ref=lattice.at[me],
            send_sem=a2a_send.at[k], recv_sem=a2a_recv.at[k],
            device_id=place(to), device_id_type=MESH,
        )

    def inward(k):
        return pltpu.make_async_remote_copy(
            src_ref=phased.at[me], dst_ref=lattice.at[(me + groups - k) % groups],
            send_sem=a2a_send.at[k], recv_sem=a2a_recv.at[k],
            device_id=place((me + k) % groups), device_id_type=MESH,
        )

    def send_out(k, carry):
        outward(k).start()
        return carry

    lax.fori_loop(1, groups, send_out, 0)
    tokens_copy = pair_copy(0, x_ref.at[pl.ds(pl.multiple_of(other * half, half), half)], rest)
    tokens_copy.start()
    lattice[me] = phased[me]

    log_scale = math.log2(math.e) / math.sqrt(size)
    lane = lax.broadcasted_iota(jnp.int32, (1, LANES), 1)

    def clear(ref, begin, count, weight):
        mark = jnp.where(lane == size, weight, 0.0).astype(jnp.bfloat16)
        mark = jnp.broadcast_to(mark, (count, LANES))
        blank = jnp.zeros((count, LANES), jnp.bfloat16)

        def body(h, carry):
            at = pl.ds(begin, count)
            if begin == 0:
                ref[h, at, :] = blank
            ref[HEADS + h, at, :] = blank
            ref[2 * HEADS + h, at, :] = mark
            return carry

        lax.fori_loop(0, HEADS, body, 0)

    def spread(ref, part, at, value):
        value = value.astype(jnp.bfloat16)
        for h in range(HEADS):
            ref[part * HEADS + h, at, 0:size] = value[:, h * size : (h + 1) * size]

    def weights_of(part):
        return w_ref[:, pl.ds(pl.multiple_of(part * width, LANES), width)]

    piece = 2 * CHUNK

    def project_all(ref, load):
        def body(step, carry):
            part = step // (tile // piece)
            i = step % (tile // piece)
            at = pl.ds(pl.multiple_of(i * piece, piece), piece)
            y = jnp.dot(load(i, at), weights_of(part), preferred_element_type=jnp.float32)
            factor = jnp.where(part == 0, log_scale, 1.0)
            spread(ref, part, at, y * factor)
            return carry

        lax.fori_loop(0, 3 * (tile // piece), body, 0)

    wide = piece // per
    clear(near, 0, tile, jnp.ones((1, 1), jnp.float32))
    clear(far, 0, tile, jnp.ones((1, 1), jnp.float32))
    w_copy.wait()
    project_all(near, lambda i, at: phased[pl.ds(i * wide, wide)].reshape(piece, width))

    offset_at = pl.ds(pl.multiple_of(row * padded, padded), padded)
    r_off = offs_ref[offset_at, 0:1]
    c_off = offs_ref[offset_at, 1:2]
    left = jnp.where(col == 0, 0, reach_ref[2])
    right = jnp.where(col == col_groups - 1, 0, reach_ref[3])
    allowed = (
        (r_off >= -reach_ref[0])
        & (r_off < rows + reach_ref[1])
        & (c_off >= -left)
        & (c_off < cols + right)
    )
    allow = jnp.where(allowed, 1.0, 0.0)
    halo_in[sent:padded, :] = jnp.zeros((padded - sent, width), jnp.bfloat16)
    clear(near, tile, padded, allow)
    for copy in halo_copies:
        copy.wait_recv()
    halo_at = pl.ds(tile, padded)

    def project_halo(part, carry):
        weight = weights_of(part)
        y = jnp.dot(halo_in[...], weight, preferred_element_type=jnp.float32)
        spare = jnp.dot(normed[0:16, :], weight, preferred_element_type=jnp.float32)[0:1, :]
        spare = spare * jnp.where(part == 1, 1.0, 0.0)
        spread(near, part, halo_at, jnp.where(allow > 0.5, y, spare))
        return carry

    lax.fori_loop(1, 3, project_halo, 0)

    def attend_heads(ref, first, last):
        keys = ref.shape[1]

        def score(h, scores):
            scores[:, 0:keys] = lax.dot_general(
                ref[h, 0:tile, :], ref[HEADS + h], (((1,), (1,)), ((), ())),
                preferred_element_type=jnp.float32,
            )

        def weigh(h, scores):
            values = ref[2 * HEADS + h]
            for r in range(tile // piece):
                at = pl.ds(r * piece, piece)
                held = scores[at, 0:keys]
                powers = jnp.exp2(held - jnp.max(held, axis=-1, keepdims=True))
                got = jnp.dot(
                    powers.astype(jnp.bfloat16), values, preferred_element_type=jnp.float32
                )
                got = got * (1.0 / got[:, size : size + 1])
                heads_out[h, at, :] = got.astype(jnp.bfloat16)

        score(first, scores_a)

        def body(i, carry):
            h = first + 2 * i
            score(h + 1, scores_b)
            weigh(h, scores_a)
            score(jnp.minimum(h + 2, last - 1), scores_a)
            weigh(h + 1, scores_b)
            return carry

        lax.fori_loop(0, (last - first) // 2, body, 0)

    def gather_heads(target, first, last):
        count = target.shape[0] * CHUNK // tile

        def body(i, carry):
            at = pl.ds(pl.multiple_of(i * CHUNK, CHUNK), CHUNK)
            to = pl.ds(i * count, count)
            for h in range(first, last):
                value = heads_out[h, at, 0:size].reshape(count, 2, per // 2, size)
                target[to, :, :, h * size : (h + 1) * size] = value
            return carry

        lax.fori_loop(0, tile // CHUNK, body, 0)

    attend_heads(near, 0, HEADS // 2)
    gather_heads(win, 0, HEADS // 2)

    def take_in(k, carry):
        inward(k).wait_recv()
        return carry

    lax.fori_loop(1, groups, take_in, 0)
    project_all(far, lambda i, at: lattice[pl.ds(i * wide, wide)].reshape(piece, width))
    attend_heads(far, 0, HEADS)
    gather_heads(dil, 0, HEADS)
    dil_copy = pair_copy(1, dil.at[:, other], dil_other)
    dil_copy.start()
    dil_copy.wait_recv()
    mine = jnp.where(branch == 1, GUIDANCE, 1.0 - GUIDANCE)
    theirs = 1.0 - mine

    def combine(i, carry):
        combined[i] = (
            mine * dil[i, branch].astype(jnp.float32) + theirs * dil_other[i].astype(jnp.float32)
        ).astype(jnp.bfloat16)
        return carry

    lax.fori_loop(0, groups, combine, 0)

    def back(k):
        to = (me + k) % groups
        return pltpu.make_async_remote_copy(
            src_ref=combined.at[to], dst_ref=returned.at[me],
            send_sem=ret_send.at[k], recv_sem=ret_recv.at[k],
            device_id=place(to), device_id_type=MESH,
        )

    def back_in(k):
        return pltpu.make_async_remote_copy(
            src_ref=combined.at[me], dst_ref=returned.at[(me + groups - k) % groups],
            send_sem=ret_send.at[k], recv_sem=ret_recv.at[k],
            device_id=place((me + k) % groups), device_id_type=MESH,
        )

    def send_back(k, carry):
        back(k).start()
        return carry

    lax.fori_loop(1, groups, send_back, 0)
    returned[me] = combined[me]

    attend_heads(near, HEADS // 2, HEADS)
    gather_heads(win, HEADS // 2, HEADS)
    win_copy = pair_copy(2, win.at[:, other], win_other)
    win_copy.start()

    def take_back(k, carry):
        back_in(k).wait_recv()
        return carry

    lax.fori_loop(1, groups, take_back, 0)
    win_copy.wait_recv()
    tokens_copy.wait_recv()

    shares = blend_ref[pl.ds(pl.multiple_of(branch * (rows // 2), rows // 2), rows // 2), :]
    r_at = offs_ref[2 * padded :, 0:1]
    c_at = offs_ref[2 * padded :, 1:2]
    weight = jnp.zeros((half, cols), jnp.float32)
    for r in range(rows // 2):
        weight = jnp.where(r_at == r, shares[r : r + 1, :], weight)
    picked = c_at == lax.broadcasted_iota(jnp.int32, (half, cols), 1)
    weight = jnp.sum(jnp.where(picked, weight, 0.0), axis=-1, keepdims=True)
    wout_copy.wait()
    window = mine * win[:, branch].astype(jnp.float32) + theirs * win_other[...].astype(jnp.float32)
    window = window.reshape(half, width)
    dilated = returned[...].astype(jnp.float32).reshape(half, width)
    mixed = (weight * window + (1.0 - weight) * dilated).astype(jnp.bfloat16)
    mixed = jnp.dot(restore_ref[...], mixed, preferred_element_type=jnp.float32)
    projected = jnp.dot(
        mixed.astype(jnp.bfloat16), wout_ref[...], preferred_element_type=jnp.float32
    )
    own = x_ref[pl.ds(pl.multiple_of(branch * half, half), half), :].astype(jnp.float32)
    base = mine * own + theirs * rest[...].astype(jnp.float32)
    out_ref[...] = (base + mod_ref[2:3, :] * projected).astype(jnp.bfloat16)

    for copy in halo_copies:
        copy.wait_send()
    for copy in (tokens_copy, dil_copy, win_copy):
        copy.wait_send()

    def finish(k, carry):
        outward(k).wait_send()
        back(k).wait_send()
        return carry

    lax.fori_loop(1, groups, finish, 0)


def on_device_fused(dims, tokens, modulation, wqkv, w_out, blend, reach):
    rows, cols, row_groups, col_groups = dims
    tile = rows * cols
    half = tile // 2
    groups = row_groups * col_groups
    per = tile // groups
    width = tokens.shape[-1]
    _, sent = halo_slots(rows, cols)
    padded = -(-(tile + sent) // LANES) * LANES - tile
    select, restore, offsets = selections(rows, cols, row_groups, col_groups, padded)
    bf16 = jnp.bfloat16
    vmem = pl.BlockSpec(memory_space=pltpu.VMEM)
    out = pl.pallas_call(
        functools.partial(fused, dims),
        out_shape=jax.ShapeDtypeStruct((half, width), bf16),
        in_specs=[vmem] * 2 + [pl.BlockSpec(memory_space=pl.ANY)] * 2 + [vmem]
        + [pl.BlockSpec(memory_space=pltpu.SMEM)] + [vmem] * 3,
        out_specs=vmem,
        scratch_shapes=[
            pltpu.VMEM((tile, width), bf16),
            pltpu.VMEM((groups, per, width), bf16),
            pltpu.VMEM((sent, width), bf16),
            pltpu.VMEM((padded, width), bf16),
            pltpu.VMEM((groups, per, width), bf16),
            pltpu.VMEM((3 * HEADS, tile + padded, LANES), bf16),
            pltpu.VMEM((3 * HEADS, tile, LANES), bf16),
            pltpu.VMEM((groups, 2, per // 2, width), bf16),
            pltpu.VMEM((groups, per // 2, width), bf16),
            pltpu.VMEM((groups, per // 2, width), bf16),
            pltpu.VMEM((groups, per // 2, width), bf16),
            pltpu.VMEM((groups, 2, per // 2, width), bf16),
            pltpu.VMEM((groups, per // 2, width), bf16),
            pltpu.VMEM((half, width), bf16),
            pltpu.VMEM(wqkv.shape, bf16),
            pltpu.VMEM(w_out.shape, bf16),
            pltpu.VMEM((tile, tile + padded), jnp.float32),
            pltpu.VMEM((tile, tile + padded), jnp.float32),
            pltpu.VMEM((HEADS, tile, LANES), bf16),
            pltpu.SemaphoreType.DMA((2,)),
            pltpu.SemaphoreType.DMA((groups,)),
            pltpu.SemaphoreType.DMA((groups,)),
            pltpu.SemaphoreType.DMA((5,)),
            pltpu.SemaphoreType.DMA((5,)),
            pltpu.SemaphoreType.DMA((groups,)),
            pltpu.SemaphoreType.DMA((groups,)),
            pltpu.SemaphoreType.DMA((3,)),
            pltpu.SemaphoreType.DMA((3,)),
        ],
        compiler_params=pltpu.CompilerParams(
            collective_id=0, has_side_effects=True, vmem_limit_bytes=60 * 1024 * 1024
        ),
    )(
        tokens.reshape(tile, width), modulation, wqkv, w_out, blend, reach.reshape(4),
        jnp.asarray(select, bf16), jnp.asarray(restore, bf16), jnp.asarray(offsets),
    )
    return out.reshape(rows // 2, cols, width)


def solution(mesh):
    in_specs = (
        P("branch", "row", "col", None),
        P(),
        P(),
        P(),
        P("row", "col"),
        P(None, "row", "col"),
    )
    out_specs = P(("row", "branch"), "col", None)
    row_groups, col_groups = mesh.shape["row"], mesh.shape["col"]

    def whole(tokens, *others):
        rows, cols = tokens.shape[1] // row_groups, tokens.shape[2] // col_groups
        groups = row_groups * col_groups
        fits = (
            row_groups == 2
            and col_groups > 2
            and (rows * cols) % (32 * groups) == 0
            and rows // row_groups % 2 == 0
            and rows % 16 == 0
        )
        body = on_device
        if fits:
            body = functools.partial(on_device_fused, (rows, cols, row_groups, col_groups))
        return jax.shard_map(
            body, mesh=mesh, in_specs=in_specs, out_specs=out_specs, check_vma=False
        )(tokens, *others)

    return whole
```
